32 devices in a mesh: group: 2 (over x), chain: 16 (over z, y, core).
Axes of the slice: x: 2, y: 2, z: 4, core: 2. Of those that a mesh axis runs over, the one named last changes fastest.
Arguments:
- separator_block: float32 [32, 512, 512], P(('group', 'chain')), parts along dimension 0, as said below
- coupling: float32 [32, 512, 512], P(('group', 'chain')), parts along dimension 0
- separator_load: float32 [32, 512, 128], P(('group', 'chain')), parts along dimension 0
- node_order: int32 [32, 512], P(('group', 'chain')), parts along dimension 0, may hold values from 0 to 511, each once within a row
- spike_left: bfloat16 [32, 1024, 512], P(('group', 'chain')), parts along dimension 0, may hold values from -0.25 to 0.25
- spike_right: bfloat16 [32, 1024, 512], P(('group', 'chain')), parts along dimension 0, may hold values from -0.25 to 0.25
- interior_local: float32 [32, 1024, 128], P(('group', 'chain')), parts along dimension 0, may hold values from -6 to 6
Outputs:
- solution: float32 [32, 512, 128], P(('group', 'chain')), parts along dimension 0
- interior: float32 [32, 1024, 128], P(('group', 'chain')), parts along dimension 0
The draws below stay inside these ranges and needn't reach their ends.
There are 2 independent parts, one for each index of `group`. The reference program is written for one: setup_inputs(seed, part) draws one part's arguments, and reference() takes and returns one part's arrays. A program takes and returns all parts, laid end to end along the dimension named above; each array names one. Nothing has to cross between parts.
Inputs may be any that keep to these rules, and one draw needn't show every extreme that they name: `separator_block`: each block is symmetric, and the matrix M of the steps is symmetric positive definite; M is not block diagonally dominant. `node_order`: each row holds every number from 0 to 511 once.
All inputs are finite; a program needn't handle non-finite values.
Results may differ from the reference program's by a relative error of at most 0.01145.
Values may be sent and summed in bfloat16 or wider, within the bound.
A program may use at most 128 MiB of HBM per device.

```python
import math
import jax
import jax.numpy as jnp
from jax import lax

B = 512
R = 128
KINT = 2
NSEP = 16


def symmetric_noise(key, spread):
    half = spread * math.sqrt(3.0) / math.sqrt(B)
    noise = jax.random.uniform(key, (NSEP, B, B), jnp.float32, -half, half)
    return (noise + jnp.swapaxes(noise, 1, 2)) * (1.0 / math.sqrt(2.0))


def edge_weights(key, spread):
    keys = jax.random.split(key, 2)
    scales = jnp.exp(jax.random.uniform(keys[0], (NSEP,), jnp.float32, math.log(0.7), math.log(2.1)))
    identity = jnp.eye(B, dtype=jnp.float32)[None]
    return scales[:, None, None] * (identity + symmetric_noise(keys[1], spread))


def draw_separator_block(key, part):
    spread = 0.25
    mass_low = 6.0
    mass_high = 18.0
    weights = edge_weights(key, spread)
    key = jax.random.fold_in(key, 11)
    keys = jax.random.split(key, 2)
    square_count = float(NSEP * NSEP)
    masses = jnp.exp(jax.random.uniform(keys[0], (NSEP,), jnp.float32, math.log(mass_low / square_count), math.log(mass_high / square_count)))
    identity = jnp.eye(B, dtype=jnp.float32)[None]
    mass_block = masses[:, None, None] * (identity + symmetric_noise(keys[1], spread))
    return weights + jnp.roll(weights, 1, axis=0) + mass_block


def draw_coupling(key, part):
    spread = 0.25
    weights = edge_weights(key, spread)
    return -weights


def draw_separator_load(key, part):
    key = jax.random.fold_in(key, 37)
    scale = 24.0 / float(NSEP) ** 1.5
    values = scale * jax.random.normal(key, (NSEP, B, R), jnp.float32)
    return values


def steps_of(stream_key, extent, cuts, smallest, largest):
    def one(position, parts):
        steps = jax.random.uniform(jax.random.fold_in(jax.random.fold_in(stream_key, 6), position), (parts,), jnp.float32, smallest / len(cuts), largest / len(cuts))
        return jnp.repeat(jnp.exp(steps), extent[position] // parts).reshape((-1,) + (1,) * (len(extent) - position - 1))

    factor_of = one(*cuts[0])
    for cut in cuts[1:]:
        factor_of = factor_of * one(*cut)
    return factor_of


def normal_values(rng, extent, scale, reach, shards=(), held_as=jnp.bfloat16):
    loudness = steps_of(rng, extent, shards, -0.22, 0.18) if shards else 1.0
    values = jax.random.normal(rng, extent, jnp.float32) * scale * loudness
    return jnp.minimum(jnp.maximum(values, -reach), reach).astype(held_as)


def setup_inputs(seed: int = 0, part: int = 0) -> dict:
    splits = jax.random.split(jax.random.key(seed), 8)
    part_splits = jax.random.split(jax.random.fold_in(splits[7], part), 8)
    separator_block = draw_separator_block(jax.random.fold_in(jax.random.fold_in(splits[7], part), 71), part)
    coupling = draw_coupling(jax.random.fold_in(jax.random.fold_in(splits[7], part), 71), part)
    separator_load = draw_separator_load(jax.random.fold_in(jax.random.fold_in(splits[7], part), 71), part)
    node_order = jax.vmap(lambda own: jax.random.permutation(own, B))(jax.random.split(part_splits[3], NSEP)).reshape((NSEP, B)).astype(jnp.int32)
    spike_left = normal_values(part_splits[4], (NSEP, KINT * B, B), B ** -0.5, 0.25, ((0, 16),))
    spike_right = normal_values(part_splits[5], (NSEP, KINT * B, B), B ** -0.5, 0.25, ((0, 16),))
    interior_local = normal_values(part_splits[6], (NSEP, KINT * B, R), 1.0, 6.0, ((0, 16),), jnp.float32)
    return dict(separator_block=separator_block, coupling=coupling, separator_load=separator_load, node_order=node_order, spike_left=spike_left, spike_right=spike_right, interior_local=interior_local)


highest = lax.Precision.HIGHEST

def reference(separator_block, coupling, separator_load, node_order, spike_left, spike_right, interior_local):
    loads = jax.vmap(lambda rows_in, order_in: rows_in[order_in])(separator_load, node_order.astype(jnp.int32))

    def forward(carry, items):
        pivot_prev, load_prev, couple_prev = carry
        diag_block, couple_now, load_now = items
        solved = jnp.linalg.solve(pivot_prev, jnp.concatenate([couple_prev, load_prev], axis=1))
        pivot_block = diag_block - jnp.dot(couple_prev.T, solved[:, :B], precision=highest)
        reduced = load_now - jnp.dot(couple_prev.T, solved[:, B:], precision=highest)
        return ((pivot_block, reduced, couple_now), (pivot_block, reduced))
    start_carry = (jnp.eye(B, dtype=jnp.float32), jnp.zeros((B, R), jnp.float32), jnp.zeros((B, B), jnp.float32))
    last_carry, stacked = lax.scan(forward, start_carry, (separator_block, coupling, loads))
    pivots, reduced_loads = stacked

    def backward(later_sol, items):
        pivot_block, load_now, couple_now = items
        result = jnp.linalg.solve(pivot_block, load_now - jnp.dot(couple_now, later_sol, precision=highest))
        return (result, result)
    first_sol, solution = lax.scan(backward, jnp.zeros((B, R), jnp.float32), (pivots, reduced_loads, coupling), reverse=True)
    prior = jnp.concatenate([jnp.zeros((1, B, R), jnp.float32), solution[:-1]], axis=0)
    prior_low = lax.optimization_barrier(prior.astype(jnp.bfloat16))
    own_low = lax.optimization_barrier(solution.astype(jnp.bfloat16))
    left_term = jnp.einsum('nkb,nbr->nkr', spike_left.astype(jnp.float32), prior_low.astype(jnp.float32))
    right_term = jnp.einsum('nkb,nbr->nkr', spike_right.astype(jnp.float32), own_low.astype(jnp.float32))
    interior = interior_local - (left_term + right_term)
    return (solution, interior)
```

```python
import functools

import jax
import jax.numpy as jnp
from jax import lax
from jax.experimental import pallas as pl
from jax.experimental.pallas import tpu as pltpu
from jax.sharding import PartitionSpec as P

F32 = jnp.float32
BF16 = jnp.bfloat16
NN = (((1,), (0,)), ((), ()))
NT = (((1,), (1,)), ((), ()))


def split(a):
    high = a.astype(BF16)
    return high, (a - high.astype(F32)).astype(BF16)


def dot1(a, b, dims=NN):
    return lax.dot_general(a, b, dims, preferred_element_type=F32)


def dot3(a, b, dims=NN):
    return dot1(a[0], b[0], dims) + (dot1(a[0], b[1], dims) + dot1(a[1], b[0], dims))


def identity(order):
    rows = lax.broadcasted_iota(jnp.int32, (order, order), 0)
    columns = lax.broadcasted_iota(jnp.int32, (order, order), 1)
    return jnp.where(rows == columns, 1.0, 0.0).astype(F32)


def newton_inverse(d_high, d_low, x_ref, start):
    order = x_ref.shape[0]

    def rough(state):
        step, size = state
        x = x_ref[...].astype(BF16)
        residual = identity(order) - dot1(d_high[...], x)
        x_ref[...] = x.astype(F32) + dot1(x, residual.astype(BF16))
        return step + 1, jnp.sum(residual * residual)

    _, size = lax.while_loop(
        lambda state: (state[0] < 30) & (state[1] > 0.1), rough, (0, jnp.float32(1e30))
    )

    @pl.when(jnp.logical_not(size <= 0.1))
    def _():
        x_ref[...] = start()

    def fine(state):
        step, size, _ = state
        x = split(x_ref[...])
        residual = identity(order) - dot3((d_high[...], d_low[...]), x)
        r = split(residual)
        x_ref[...] = x_ref[...] + (dot1(x[0], r[0]) + (dot1(x[1], r[0]) + dot1(x[0], r[1])))
        return step + 1, jnp.sum(residual * residual), size

    def going(state):
        step, size, before = state
        stalled = (size < 0.1) & (size > 0.25 * before)
        return (step < 60) & (size > 1e-5) & jnp.logical_not(stalled)

    lax.while_loop(going, fine, (0, jnp.float32(1e30), jnp.float32(1e30)))


def inverse_kernel(first, *refs):
    if first:
        d_ref, load_ref, order_ref, v_ref, g_ref, b_out, d_high, d_low = refs
        size = load_ref.shape[0]
        d = d_ref[...]
        places = lax.broadcasted_iota(jnp.int32, (size, size), 0)
        chosen = jnp.where(places == order_ref[...], 1.0, 0.0).astype(BF16)
        load = load_ref[...]
        high = load.astype(BF16)
        rest = load - high.astype(F32)
        middle = rest.astype(BF16)
        low = (rest - middle.astype(F32)).astype(BF16)
        take = (((0,), (0,)), ((), ()))
        b = dot1(chosen, high, take) + (dot1(chosen, middle, take) + dot1(chosen, low, take))
    else:
        d_ref, b_ref, right_ref, left_ref, v_ref, g_ref, d_out, b_out, d_high, d_low = refs
        size = b_ref.shape[0]
        d = d_ref[...] - (right_ref[:, :size] + left_ref[:, :size])
        b = b_ref[...] - (right_ref[:, size:] + left_ref[:, size:])
        d_out[...] = d
    b_out[...] = b
    d_high[...], d_low[...] = split(d)
    scale = 1.0 / jnp.max(jnp.sum(jnp.abs(d), axis=1))

    def start():
        whole = d_high[...].astype(F32) + d_low[...].astype(F32)
        return scale * (2.0 * identity(size) - scale * whole)

    v_ref[...] = start()
    newton_inverse(d_high, d_low, v_ref, start)
    g_ref[...] = dot3(split(v_ref[...]), split(b_out[...]))


def update_kernel(first, v_ref, g_ref, left_ref, right_ref, to_left, to_right, *rest):
    size = v_ref.shape[0]
    v = split(v_ref[...])
    g = split(g_ref[...])
    right = right_ref[...]
    if first:
        right = right.T
        rest[0][...] = right
    for coupling, out in ((right, to_right), (left_ref[...], to_left)):
        u = split(coupling)
        w = split(dot3(u, v))
        out[:, :size] = dot3(w, u, NT)
        out[:, size:] = dot3(u, g)


def couple_kernel(passed, v_ref, left_ref, right_ref, h_ref, m_ref, *rest):
    v = split(v_ref[...])
    left = split(left_ref[...])
    right = split(right_ref[...])
    h = dot3(v, left, NT)
    m = dot3(v, right, NT)
    h_ref[...] = h
    m_ref[...] = m
    if passed:
        onward, back = rest
        onward[...] = -dot3(left, split(m))
        back[...] = -dot3(right, split(h))


def back_kernel(x_ref, g_ref, h_ref, m_ref, left_ref, right_ref, out_ref):
    out_ref[...] = g_ref[...] - (
        dot3(split(h_ref[...]), split(left_ref[...]))
        + dot3(split(m_ref[...]), split(right_ref[...]))
    )


def call(kernel, out_shape, *operands, scratch=(), flops=0):
    return pl.pallas_call(
        kernel,
        out_shape=out_shape,
        in_specs=[pl.BlockSpec(memory_space=pltpu.VMEM)] * len(operands),
        out_specs=jax.tree.map(lambda _: pl.BlockSpec(memory_space=pltpu.VMEM), out_shape),
        scratch_shapes=list(scratch),
        compiler_params=pltpu.CompilerParams(vmem_limit_bytes=48 * 2**20),
        cost_estimate=pl.CostEstimate(flops=flops, bytes_accessed=4 * 2**20, transcendentals=0),
    )(*operands)


def send(block, distance, senders, devices):
    route = [(i, i + distance) for i in senders if 0 <= i + distance < devices]
    return lax.ppermute(block, "chain", route)


def plan(devices):
    levels = []
    stride = 1
    while devices // stride > 4:
        gone = list(range(stride, devices, 2 * stride))
        left = list(range(0, devices, 2 * stride))
        if len(left) > 4:
            next_gone = set(left[1::2])
            rightward = [i for i in gone if i + stride in next_gone]
            leftward = [i for i in gone if i - stride in next_gone]
        else:
            leftward = [left[0] + stride, left[1] + stride]
            rightward = [left[1] + stride, left[2] + stride]
        levels.append((stride, gone, rightward, leftward))
        stride *= 2
    levels.append((stride, [0, 3 * stride], [], []))
    levels.append((stride, [stride, 2 * stride], [], []))
    return levels


def among(position, members):
    hit = position == members[0]
    for member in members[1:]:
        hit = hit | (position == member)
    return hit


def per_device(
    separator_block, coupling, separator_load, node_order, spike_left, spike_right, interior_local
):
    devices = lax.axis_size("chain")
    position = lax.axis_index("chain")
    size = separator_block.shape[1]
    wide = separator_load.shape[2]
    square = jax.ShapeDtypeStruct((size, size), F32)
    thin = jax.ShapeDtypeStruct((size, wide), F32)
    payload = jax.ShapeDtypeStruct((size, size + wide), F32)
    halves = (pltpu.VMEM((size, size), BF16),) * 2
    cube = 2 * size**3

    d = separator_block[0]
    right = jnp.where(position == devices - 1, 0.0, coupling[0])
    levels = plan(devices)
    left = send(right, 1, [i - 1 for i in levels[0][1]], devices)
    kept = []
    b = None
    for index, (stride, gone, rightward, leftward) in enumerate(levels):
        first = index == 0
        last = index == len(levels) - 1
        if first:
            v, g, b = call(
                functools.partial(inverse_kernel, True),
                (square, thin, thin),
                d,
                separator_load[0],
                node_order.reshape(1, size),
                scratch=halves,
                flops=25 * cube,
            )
        else:
            v, g, d, b = call(
                functools.partial(inverse_kernel, False),
                (square, thin, square, thin),
                d,
                b,
                from_right,
                from_left,
                scratch=halves,
                flops=25 * cube,
            )
        outs = call(
            functools.partial(update_kernel, first),
            (payload, payload) + ((square,) if first else ()),
            v,
            g,
            left,
            right,
            flops=14 * cube,
        )
        to_left, to_right = outs[:2]
        if first:
            right = outs[2]
        if last:
            from_right = send(to_left, -stride, [gone[1]], devices)
            from_left = send(to_right, stride, [gone[0]], devices)
            break
        if len(gone) == 2 and gone[0] == 0:
            from_right = send(to_left, -stride, [gone[1]], devices)
            from_left = send(to_right, stride, [gone[0]], devices)
        else:
            from_right = send(to_left, -stride, gone, devices)
            from_left = send(to_right, stride, gone, devices)
        passed = bool(rightward)
        outs = call(
            functools.partial(couple_kernel, passed),
            (square, square) + ((square, square) if passed else ()),
            v,
            left,
            right,
            flops=12 * cube,
        )
        kept.append((g, outs[0], outs[1], stride, gone))
        if passed:
            new_left = send(outs[2], stride, rightward, devices)
            new_right = send(outs[3], -stride, leftward, devices)
            left = new_left
            right = new_right

    _, x, _, _ = call(
        functools.partial(inverse_kernel, False),
        (square, thin, square, thin),
        d,
        b,
        from_right,
        from_left,
        scratch=halves,
        flops=25 * cube,
    )
    for g, h, m, stride, gone in reversed(kept):
        x_left = send(x, stride, [i - stride for i in gone if i >= stride], devices)
        x_right = send(x, -stride, [i + stride for i in gone if i + stride < devices], devices)
        found = call(back_kernel, thin, x, g, h, m, x_left, x_right, flops=3 * cube // 2)
        x = jnp.where(among(position, gone), found, x)
    own_low = x.astype(BF16)
    prior_low = send(own_low, 1, range(devices - 1), devices)
    left_term = jnp.dot(spike_left[0], prior_low, preferred_element_type=F32)
    right_term = jnp.dot(spike_right[0], own_low, preferred_element_type=F32)
    interior = interior_local[0] - (left_term + right_term)
    return (x[None], interior[None])


def solution(mesh):
    blocks = P(("group", "chain"), None, None)
    placed = (blocks, blocks, blocks, P(("group", "chain"), None), blocks, blocks, blocks)
    return jax.shard_map(
        per_device, mesh=mesh, in_specs=placed, out_specs=(blocks, blocks), check_vma=False
    )
```

```python
import functools

import jax
import jax.numpy as jnp
from jax import lax
from jax.experimental import pallas as pl
from jax.experimental.pallas import tpu as pltpu
from jax.sharding import PartitionSpec as P

F32 = jnp.float32
BF16 = jnp.bfloat16
NN = (((1,), (0,)), ((), ()))
NT = (((1,), (1,)), ((), ()))


def split(a):
    high = a.astype(BF16)
    return high, (a - high.astype(F32)).astype(BF16)


def dot1(a, b, dims=NN):
    return lax.dot_general(a, b, dims, preferred_element_type=F32)


def dot3(a, b, dims=NN):
    return dot1(a[0], b[0], dims) + (dot1(a[0], b[1], dims) + dot1(a[1], b[0], dims))


def identity(order):
    rows = lax.broadcasted_iota(jnp.int32, (order, order), 0)
    columns = lax.broadcasted_iota(jnp.int32, (order, order), 1)
    return jnp.where(rows == columns, 1.0, 0.0).astype(F32)


def newton_inverse(d_high, d_low, x_ref, start):
    order = x_ref.shape[0]

    def rough(state):
        step, size = state
        x = x_ref[...].astype(BF16)
        residual = identity(order) - dot1(d_high[...], x)
        x_ref[...] = x.astype(F32) + dot1(x, residual.astype(BF16))
        return step + 1, jnp.sum(residual * residual)

    _, size = lax.while_loop(
        lambda state: (state[0] < 30) & (state[1] > 2.0), rough, (0, jnp.float32(1e30))
    )

    @pl.when(jnp.logical_not(size <= 2.0))
    def _():
        x_ref[...] = start()

    def fine(state):
        step, size, _ = state
        x = split(x_ref[...])
        residual = identity(order) - dot3((d_high[...], d_low[...]), x)
        now = jnp.sum(residual * residual)
        r = residual.astype(BF16)

        @pl.when(now > 1.0)
        def _():
            y = split(residual)
            x_ref[...] = x_ref[...] + (dot1(x[0], y[0]) + (dot1(x[1], y[0]) + dot1(x[0], y[1])))

        @pl.when(now <= 1.0)
        def _():
            square = dot1(r, r)
            total = residual + square + dot1(r, square.astype(BF16))
            x_ref[...] = x_ref[...] + dot1(x[0], total.astype(BF16))

        return step + 1, now, size

    def going(state):
        step, size, before = state
        stalled = (size < 0.1) & (size > 0.25 * before)
        return (step < 60) & (size > 0.02) & jnp.logical_not(stalled)

    lax.while_loop(going, fine, (0, jnp.float32(1e30), jnp.float32(1e30)))


T = 128


def upper_blocks(count):
    return [(i, j) for i in range(count) for j in range(i, count)]


def pack(out, w, u, thin):
    size = thin.shape[0]
    slot = 0
    for i in range(size // T):
        rows = slice(i * T, (i + 1) * T)
        strip = dot3((w[0][rows], w[1][rows]), (u[0][i * T :], u[1][i * T :]), NT)
        for j in range(i, size // T):
            out[slot * T : (slot + 1) * T, :] = strip[:, (j - i) * T : (j - i + 1) * T]
            slot += 1
    out[slot * T :, :] = thin


def subtract_packed(d_ref, right_ref, left_ref, d_out):
    count = d_ref.shape[0] // T
    for slot, (i, j) in enumerate(upper_blocks(count)):
        here = slice(slot * T, (slot + 1) * T)
        block = right_ref[here, :] + left_ref[here, :]
        rows, columns = slice(i * T, (i + 1) * T), slice(j * T, (j + 1) * T)
        d_out[rows, columns] = d_ref[rows, columns] - block
        if i != j:
            d_out[columns, rows] = d_ref[columns, rows] - block.T
    return (slot + 1) * T


def inverse_kernel(first, *refs):
    if first:
        d_ref, load_ref, order_ref, v_ref, g_ref, b_out, d_high, d_low = refs
        size = load_ref.shape[0]
        d = d_ref[...]
        places = lax.broadcasted_iota(jnp.int32, (size, size), 0)
        chosen = jnp.where(places == order_ref[...], 1.0, 0.0).astype(BF16)
        load = load_ref[...]
        high = load.astype(BF16)
        rest = load - high.astype(F32)
        middle = rest.astype(BF16)
        low = (rest - middle.astype(F32)).astype(BF16)
        take = (((0,), (0,)), ((), ()))
        b = dot1(chosen, high, take) + (dot1(chosen, middle, take) + dot1(chosen, low, take))
    else:
        d_ref, b_ref, right_ref, left_ref, v_ref, g_ref, d_out, b_out, d_high, d_low = refs
        size = b_ref.shape[0]
        end = subtract_packed(d_ref, right_ref, left_ref, d_out)
        d = d_out[...]
        b = b_ref[...] - (right_ref[end:, :] + left_ref[end:, :])
    b_out[...] = b
    d_high[...], d_low[...] = split(d)
    scale = 1.9 / jnp.max(jnp.sum(jnp.abs(d), axis=1))

    def start():
        whole = d_high[...].astype(F32) + d_low[...].astype(F32)
        return scale * (2.0 * identity(size) - scale * whole)

    v_ref[...] = start()
    newton_inverse(d_high, d_low, v_ref, start)
    g_ref[...] = dot3(split(v_ref[...]), split(b_out[...]))


def update_kernel(first, v_ref, g_ref, left_ref, right_ref, to_left, to_right, *rest):
    size = v_ref.shape[0]
    v = split(v_ref[...])
    g = split(g_ref[...])
    right = right_ref[...]
    if first:
        right = right.T
        rest[0][...] = right
    for coupling, out in ((right, to_right), (left_ref[...], to_left)):
        u = split(coupling)
        w = split(dot3(u, v))
        pack(out, w, u, dot3(u, g))


def couple_kernel(passed, v_ref, left_ref, right_ref, h_ref, m_ref, *rest):
    v = split(v_ref[...])
    left = split(left_ref[...])
    right = split(right_ref[...])
    h = dot3(v, left, NT)
    m = dot3(v, right, NT)
    h_ref[...] = h
    m_ref[...] = m
    if passed:
        onward, back = rest
        onward[...] = -dot3(left, split(m))
        back[...] = -dot3(right, split(h))


def back_kernel(x_ref, g_ref, h_ref, m_ref, left_ref, right_ref, out_ref):
    out_ref[...] = g_ref[...] - (
        dot3(split(h_ref[...]), split(left_ref[...]))
        + dot3(split(m_ref[...]), split(right_ref[...]))
    )


def call(kernel, out_shape, *operands, scratch=(), flops=0):
    return pl.pallas_call(
        kernel,
        out_shape=out_shape,
        in_specs=[pl.BlockSpec(memory_space=pltpu.VMEM)] * len(operands),
        out_specs=jax.tree.map(lambda _: pl.BlockSpec(memory_space=pltpu.VMEM), out_shape),
        scratch_shapes=list(scratch),
        compiler_params=pltpu.CompilerParams(vmem_limit_bytes=48 * 2**20),
        cost_estimate=pl.CostEstimate(flops=flops, bytes_accessed=4 * 2**20, transcendentals=0),
    )(*operands)


def send(block, distance, senders, devices):
    route = [(i, i + distance) for i in senders if 0 <= i + distance < devices]
    return lax.ppermute(block, "chain", route)


def plan(devices):
    levels = []
    stride = 1
    while devices // stride > 4:
        gone = list(range(stride, devices, 2 * stride))
        left = list(range(0, devices, 2 * stride))
        if len(left) > 4:
            next_gone = set(left[1::2])
            rightward = [i for i in gone if i + stride in next_gone]
            leftward = [i for i in gone if i - stride in next_gone]
        else:
            leftward = [left[0] + stride, left[1] + stride]
            rightward = [left[1] + stride, left[2] + stride]
        levels.append((stride, gone, rightward, leftward))
        stride *= 2
    levels.append((stride, [0, 3 * stride], [], []))
    levels.append((stride, [stride, 2 * stride], [], []))
    return levels


def among(position, members):
    hit = position == members[0]
    for member in members[1:]:
        hit = hit | (position == member)
    return hit


def per_device(
    separator_block, coupling, separator_load, node_order, spike_left, spike_right, interior_local
):
    devices = lax.axis_size("chain")
    position = lax.axis_index("chain")
    size = separator_block.shape[1]
    wide = separator_load.shape[2]
    square = jax.ShapeDtypeStruct((size, size), F32)
    thin = jax.ShapeDtypeStruct((size, wide), F32)
    payload = jax.ShapeDtypeStruct((len(upper_blocks(size // T)) * T + size, wide), F32)
    halves = (pltpu.VMEM((size, size), BF16),) * 2
    cube = 2 * size**3

    d = separator_block[0]
    right = jnp.where(position == devices - 1, 0.0, coupling[0])
    levels = plan(devices)
    left = send(right, 1, [i - 1 for i in levels[0][1]], devices)
    kept = []
    b = None
    for index, (stride, gone, rightward, leftward) in enumerate(levels):
        first = index == 0
        last = index == len(levels) - 1
        if first:
            v, g, b = call(
                functools.partial(inverse_kernel, True),
                (square, thin, thin),
                d,
                separator_load[0],
                node_order.reshape(1, size),
                scratch=halves,
                flops=25 * cube,
            )
        else:
            v, g, d, b = call(
                functools.partial(inverse_kernel, False),
                (square, thin, square, thin),
                d,
                b,
                from_right,
                from_left,
                scratch=halves,
                flops=25 * cube,
            )
        outs = call(
            functools.partial(update_kernel, first),
            (payload, payload) + ((square,) if first else ()),
            v,
            g,
            left,
            right,
            flops=14 * cube,
        )
        to_left, to_right = outs[:2]
        if first:
            right = outs[2]
        if last:
            from_right = send(to_left, -stride, [gone[1]], devices)
            from_left = send(to_right, stride, [gone[0]], devices)
            break
        if len(gone) == 2 and gone[0] == 0:
            from_right = send(to_left, -stride, [gone[1]], devices)
            from_left = send(to_right, stride, [gone[0]], devices)
        else:
            from_right = send(to_left, -stride, gone, devices)
            from_left = send(to_right, stride, gone, devices)
        passed = bool(rightward)
        outs = call(
            functools.partial(couple_kernel, passed),
            (square, square) + ((square, square) if passed else ()),
            v,
            left,
            right,
            flops=12 * cube,
        )
        kept.append((g, outs[0], outs[1], stride, gone))
        if passed:
            new_left = send(outs[2], stride, rightward, devices)
            new_right = send(outs[3], -stride, leftward, devices)
            left = new_left
            right = new_right

    _, x, _, _ = call(
        functools.partial(inverse_kernel, False),
        (square, thin, square, thin),
        d,
        b,
        from_right,
        from_left,
        scratch=halves,
        flops=25 * cube,
    )
    for g, h, m, stride, gone in reversed(kept):
        x_left = send(x, stride, [i - stride for i in gone if i >= stride], devices)
        x_right = send(x, -stride, [i + stride for i in gone if i + stride < devices], devices)
        found = call(back_kernel, thin, x, g, h, m, x_left, x_right, flops=3 * cube // 2)
        x = jnp.where(among(position, gone), found, x)
    own_low = x.astype(BF16)
    prior_low = send(own_low, 1, range(devices - 1), devices)
    left_term = jnp.dot(spike_left[0], prior_low, preferred_element_type=F32)
    right_term = jnp.dot(spike_right[0], own_low, preferred_element_type=F32)
    interior = interior_local[0] - (left_term + right_term)
    return (x[None], interior[None])


def solution(mesh):
    blocks = P(("group", "chain"), None, None)
    placed = (blocks, blocks, blocks, P(("group", "chain"), None), blocks, blocks, blocks)
    return jax.shard_map(
        per_device, mesh=mesh, in_specs=placed, out_specs=(blocks, blocks), check_vma=False
    )
```

```python
import functools

import jax
import jax.numpy as jnp
from jax import lax
from jax.experimental import pallas as pl
from jax.experimental.pallas import tpu as pltpu
from jax.sharding import PartitionSpec as P

F32 = jnp.float32
BF16 = jnp.bfloat16
NN = (((1,), (0,)), ((), ()))
NT = (((1,), (1,)), ((), ()))


def split(a):
    high = a.astype(BF16)
    return high, (a - high.astype(F32)).astype(BF16)


def dot1(a, b, dims=NN):
    return lax.dot_general(a, b, dims, preferred_element_type=F32)


def dot3(a, b, dims=NN):
    return dot1(a[0], b[0], dims) + (dot1(a[0], b[1], dims) + dot1(a[1], b[0], dims))


def identity(order):
    rows = lax.broadcasted_iota(jnp.int32, (order, order), 0)
    columns = lax.broadcasted_iota(jnp.int32, (order, order), 1)
    return jnp.where(rows == columns, 1.0, 0.0).astype(F32)


def newton_inverse(d_high, d_low, x_ref, start):
    order = x_ref.shape[0]

    def rough(state):
        step, size = state
        x = x_ref[...].astype(BF16)
        residual = identity(order) - dot1(d_high[...], x)
        x_ref[...] = x.astype(F32) + dot1(x, residual.astype(BF16))
        return step + 1, jnp.sum(residual * residual)

    _, size = lax.while_loop(
        lambda state: (state[0] < 30) & (state[1] > 2.0), rough, (0, jnp.float32(1e30))
    )

    @pl.when(jnp.logical_not(size <= 2.0))
    def _():
        x_ref[...] = start()

    def fine(state):
        step, size, _ = state
        x = split(x_ref[...])
        residual = identity(order) - dot3((d_high[...], d_low[...]), x)
        now = jnp.sum(residual * residual)
        r = residual.astype(BF16)

        @pl.when(now > 1.0)
        def _():
            y = split(residual)
            x_ref[...] = x_ref[...] + (dot1(x[0], y[0]) + (dot1(x[1], y[0]) + dot1(x[0], y[1])))

        @pl.when(now <= 1.0)
        def _():
            square = dot1(r, r)
            series = residual + square + dot1(r, square.astype(BF16))
            x_ref[...] = x_ref[...] + dot1(x[0], series.astype(BF16))

        return step + 1, now, size

    def going(state):
        step, size, before = state
        stalled = (size < 0.1) & (size > 0.25 * before)
        return (step < 60) & (size > 0.02) & jnp.logical_not(stalled)

    lax.while_loop(going, fine, (0, jnp.float32(1e30), jnp.float32(1e30)))


T = 128


def upper_blocks(count):
    return [(i, j) for i in range(count) for j in range(i, count)]


def pack(out, w, u, thin):
    size = thin.shape[0]
    slot = 0
    for i in range(size // T):
        rows = slice(i * T, (i + 1) * T)
        strip = dot3((w[0][rows], w[1][rows]), (u[0][i * T :], u[1][i * T :]), NT)
        for j in range(i, size // T):
            out[slot * T : (slot + 1) * T, :] = strip[:, (j - i) * T : (j - i + 1) * T]
            slot += 1
    out[slot * T :, :] = thin


def total(updates, rows):
    out = updates[0][rows, :]
    for update in updates[1:]:
        out = out + update[rows, :]
    return out


def subtract_packed(d_ref, updates, d_out):
    count = d_ref.shape[0] // T
    for slot, (i, j) in enumerate(upper_blocks(count)):
        here = slice(slot * T, (slot + 1) * T)
        block = total(updates, here)
        rows, columns = slice(i * T, (i + 1) * T), slice(j * T, (j + 1) * T)
        d_out[rows, columns] = d_ref[rows, columns] - block
        if i != j:
            d_out[columns, rows] = d_ref[columns, rows] - block.T
    return (slot + 1) * T


def inverse_kernel(first, *refs):
    if first:
        d_ref, load_ref, order_ref, v_ref, g_ref, b_out, d_high, d_low = refs
        size = load_ref.shape[0]
        d = d_ref[...]
        places = lax.broadcasted_iota(jnp.int32, (size, size), 0)
        chosen = jnp.where(places == order_ref[...], 1.0, 0.0).astype(BF16)
        load = load_ref[...]
        high = load.astype(BF16)
        rest = load - high.astype(F32)
        middle = rest.astype(BF16)
        low = (rest - middle.astype(F32)).astype(BF16)
        take = (((0,), (0,)), ((), ()))
        b = dot1(chosen, high, take) + (dot1(chosen, middle, take) + dot1(chosen, low, take))
    else:
        d_ref, b_ref, *updates, v_ref, g_ref, d_out, b_out, d_high, d_low = refs
        size = b_ref.shape[0]
        end = subtract_packed(d_ref, updates, d_out)
        d = d_out[...]
        b = b_ref[...] - total(updates, slice(end, None))
    b_out[...] = b
    d_high[...], d_low[...] = split(d)
    scale = 1.9 / jnp.max(jnp.sum(jnp.abs(d), axis=1))

    def start():
        whole = d_high[...].astype(F32) + d_low[...].astype(F32)
        return scale * (2.0 * identity(size) - scale * whole)

    v_ref[...] = start()
    newton_inverse(d_high, d_low, v_ref, start)
    g_ref[...] = dot3(split(v_ref[...]), split(b_out[...]))


def update_kernel(first, v_ref, g_ref, left_ref, right_ref, to_left, to_right, *rest):
    size = v_ref.shape[0]
    v = split(v_ref[...])
    g = split(g_ref[...])
    right = right_ref[...]
    if first:
        at_end = lax.axis_index("chain") == lax.axis_size("chain") - 1
        right = jnp.where(at_end, 0.0, right.T)
        rest[0][...] = right
    for coupling, out in ((right, to_right), (left_ref[...], to_left)):
        u = split(coupling)
        w = split(dot3(u, v))
        pack(out, w, u, dot3(u, g))


def couple_kernel(passed, v_ref, left_ref, right_ref, h_ref, m_ref, *rest):
    v = split(v_ref[...])
    left = split(left_ref[...])
    right = split(right_ref[...])
    h = dot3(v, left, NT)
    m = dot3(v, right, NT)
    h_ref[...] = h
    m_ref[...] = m
    if passed:
        onward, back = rest
        onward[...] = -dot3(left, split(m))
        back[...] = -dot3(right, split(h))


def sweep_kernel(strides, devices, *refs):
    count = len(strides)
    x_in = refs[0]
    kept = [refs[1 + 3 * k : 4 + 3 * k] for k in range(count)]
    spike_left, spike_right, local, x_ref, out_ref = refs[1 + 3 * count : 6 + 3 * count]
    slots, own, given, send_sem, recv_sem = refs[6 + 3 * count :]
    me = lax.axis_index("chain")

    def along(distance):
        return lax.rem(me + (distance + devices), devices)

    def roles(k):
        stride, at_ends = strides[k]
        if at_ends:
            return me == 3 * stride, me == 0, me == 2 * stride, me == stride
        place = lax.rem(me, 2 * stride)
        gone, stays = place == stride, place == 0
        return gone, gone & (me + stride < devices), stays, stays & (me >= stride)

    def copies(k):
        stride = strides[k][0]
        rightward = pltpu.make_async_remote_copy(
            x_ref,
            slots.at[2 * k],
            send_sem.at[2 * k],
            recv_sem.at[2 * k],
            device_id={"chain": along(stride)},
            device_id_type=pl.DeviceIdType.MESH,
        )
        leftward = pltpu.make_async_remote_copy(
            x_ref,
            slots.at[2 * k + 1],
            send_sem.at[2 * k + 1],
            recv_sem.at[2 * k + 1],
            device_id={"chain": along(-stride)},
            device_id_type=pl.DeviceIdType.MESH,
        )
        return rightward, leftward

    round_copy = pltpu.make_async_remote_copy(
        own,
        given,
        send_sem.at[2 * count],
        recv_sem.at[2 * count],
        device_id={"chain": along(1)},
        device_id_type=pl.DeviceIdType.MESH,
    )
    x_ref[...] = x_in[...]
    slots[...] = jnp.zeros_like(slots)
    barrier = pltpu.get_barrier_semaphore()
    partners = jnp.int32(0)
    for k in range(count):
        takes_left, takes_right, gives_right, gives_left = roles(k)
        stride = strides[k][0]
        for meets, distance in ((takes_left | gives_left, -stride), (takes_right | gives_right, stride)):
            partners = partners + meets.astype(jnp.int32)

            @pl.when(meets)
            def _():
                pl.semaphore_signal(
                    barrier,
                    inc=1,
                    device_id={"chain": along(distance)},
                    device_id_type=pl.DeviceIdType.MESH,
                )

    pl.semaphore_wait(barrier, partners)
    for k in reversed(range(count)):
        takes_left, takes_right, gives_right, gives_left = roles(k)
        rightward, leftward = copies(k)
        pl.when(gives_right)(rightward.start)
        pl.when(gives_left)(leftward.start)
        pl.when(takes_left)(rightward.wait_recv)
        pl.when(takes_right)(leftward.wait_recv)
        g_ref, h_ref, m_ref = kept[k]

        @pl.when(takes_left | takes_right)
        def _():
            x_ref[...] = g_ref[...] - (
                dot3(split(h_ref[...]), split(slots[2 * k]))
                + dot3(split(m_ref[...]), split(slots[2 * k + 1]))
            )

    own[...] = x_ref[...].astype(BF16)
    odd = lax.rem(me, 2) == 1
    gives, takes = odd & (me < devices - 1), jnp.logical_not(odd) & (me > 0)
    pl.when(gives)(round_copy.start)
    out_ref[...] = dot1(spike_right[...], own[...])

    @pl.when(odd)
    def _():
        given[...] = slots[0].astype(BF16)

    @pl.when(me == 0)
    def _():
        given[...] = jnp.zeros_like(given)

    pl.when(takes)(round_copy.wait_recv)
    out_ref[...] = local[...] - (dot1(spike_left[...], given[...]) + out_ref[...])
    pl.when(gives)(round_copy.wait_send)
    for k in range(count):
        _, _, gives_right, gives_left = roles(k)
        rightward, leftward = copies(k)
        pl.when(gives_right)(rightward.wait_send)
        pl.when(gives_left)(leftward.wait_send)


def call(kernel, out_shape, *operands, scratch=(), flops=0, **params):
    return pl.pallas_call(
        kernel,
        out_shape=out_shape,
        in_specs=[pl.BlockSpec(memory_space=pltpu.VMEM)] * len(operands),
        out_specs=jax.tree.map(lambda _: pl.BlockSpec(memory_space=pltpu.VMEM), out_shape),
        scratch_shapes=list(scratch),
        compiler_params=pltpu.CompilerParams(vmem_limit_bytes=48 * 2**20, **params),
        cost_estimate=pl.CostEstimate(flops=flops, bytes_accessed=4 * 2**20, transcendentals=0),
    )(*operands)


def send(block, distance, senders, devices):
    route = [(i, i + distance) for i in senders if 0 <= i + distance < devices]
    return lax.ppermute(block, "chain", route)


def plan(devices):
    levels = []
    stride = 1
    while devices // stride > 4:
        levels.append((stride, list(range(stride, devices, 2 * stride))))
        stride *= 2
    return levels, stride


def per_device(
    separator_block, coupling, separator_load, node_order, spike_left, spike_right, interior_local
):
    devices = lax.axis_size("chain")
    size = separator_block.shape[1]
    wide = separator_load.shape[2]
    square = jax.ShapeDtypeStruct((size, size), F32)
    thin = jax.ShapeDtypeStruct((size, wide), F32)
    payload = jax.ShapeDtypeStruct((len(upper_blocks(size // T)) * T + size, wide), F32)
    halves = (pltpu.VMEM((size, size), BF16),) * 2
    cube = 2 * size**3

    d = separator_block[0]
    right = coupling[0]
    levels, top = plan(devices)
    left = send(right, 1, [i - 1 for i in levels[0][1]], devices)

    def invert(d, b, updates):
        return call(
            functools.partial(inverse_kernel, False),
            (square, thin, square, thin),
            d,
            b,
            *updates,
            scratch=halves,
            flops=16 * cube,
        )

    def update(first, v, g, left, right):
        return call(
            functools.partial(update_kernel, first),
            (payload, payload) + ((square,) if first else ()),
            v,
            g,
            left,
            right,
            flops=12 * cube,
        )

    def couple(passed, v, left, right):
        return call(
            functools.partial(couple_kernel, passed),
            (square, square) + ((square, square) if passed else ()),
            v,
            left,
            right,
            flops=12 * cube,
        )

    kept = []
    b = None
    updates = ()
    for index, (stride, gone) in enumerate(levels):
        first = index == 0
        if first:
            v, g, b = call(
                functools.partial(inverse_kernel, True),
                (square, thin, thin),
                d,
                separator_load[0],
                node_order.reshape(1, size),
                scratch=halves,
                flops=16 * cube,
            )
        else:
            v, g, d, b = invert(d, b, updates)
        outs = update(first, v, g, left, right)
        to_left, to_right = outs[:2]
        if first:
            right = outs[2]
        before_top = 2 * stride == top
        if before_top:
            urgent_left, urgent_right = [gone[0], gone[1], gone[3]], [gone[1], gone[2]]
            coupled_right, coupled_left = [gone[1], gone[2]], [gone[0], gone[1]]
        else:
            urgent_left, urgent_right = gone, gone
            coupled_right, coupled_left = gone[0::2], gone[1::2]
        updates = (
            send(to_left, -stride, urgent_left, devices),
            send(to_right, stride, urgent_right, devices),
        )
        h, m, onward, back = couple(True, v, left, right)
        kept.append((g, h, m))
        onward, back, *updates = lax.optimization_barrier((onward, back, *updates))
        left = send(onward, stride, coupled_right, devices)
        right = send(back, -stride, coupled_left, devices)

    left, right, to_left, to_right = lax.optimization_barrier((left, right, to_left, to_right))
    later = (
        send(to_left, -(top // 2), [5 * top // 2], devices),
        send(to_right, top // 2, [top // 2], devices),
    )
    v, g, d, b = invert(d, b, updates)
    to_left, to_right = update(False, v, g, left, right)
    updates = (
        send(to_left, -top, [3 * top], devices),
        send(to_right, top, [0], devices),
    )
    h, m = couple(False, v, left, right)
    kept.append((g, h, m))

    v, g, d, b = invert(d, b, (*later, *updates))
    to_left, to_right = update(False, v, g, left, right)
    updates = (
        send(to_left, -top, [2 * top], devices),
        send(to_right, top, [top], devices),
    )
    _, x, _, _ = invert(d, b, updates)

    strides = [(stride, False) for stride, _ in levels] + [(top, True)]
    tall = interior_local.shape[1]
    x, interior = call(
        functools.partial(sweep_kernel, strides, devices),
        (thin, jax.ShapeDtypeStruct((tall, wide), F32)),
        x,
        *(array for entry in kept for array in entry),
        spike_left[0],
        spike_right[0],
        interior_local[0],
        scratch=(
            pltpu.VMEM((2 * len(strides), size, wide), F32),
            pltpu.VMEM((size, wide), BF16),
            pltpu.VMEM((size, wide), BF16),
            pltpu.SemaphoreType.DMA((2 * len(strides) + 1,)),
            pltpu.SemaphoreType.DMA((2 * len(strides) + 1,)),
        ),
        flops=6 * cube,
        collective_id=0,
        has_side_effects=True,
    )
    return (x[None], interior[None])


def solution(mesh):
    blocks = P(("group", "chain"), None, None)
    placed = (blocks, blocks, blocks, P(("group", "chain"), None), blocks, blocks, blocks)
    return jax.shard_map(
        per_device, mesh=mesh, in_specs=placed, out_specs=(blocks, blocks), check_vma=False
    )
```

```python
import functools

import jax
import jax.numpy as jnp
from jax import lax
from jax.experimental import pallas as pl
from jax.experimental.pallas import tpu as pltpu
from jax.sharding import PartitionSpec as P

F32 = jnp.float32
BF16 = jnp.bfloat16
NN = (((1,), (0,)), ((), ()))
NT = (((1,), (1,)), ((), ()))


def split(a):
    high = a.astype(BF16)
    return high, (a - high.astype(F32)).astype(BF16)


def dot1(a, b, dims=NN):
    return lax.dot_general(a, b, dims, preferred_element_type=F32)


def dot3(a, b, dims=NN):
    return dot1(a[0], b[0], dims) + (dot1(a[0], b[1], dims) + dot1(a[1], b[0], dims))


def identity(order):
    rows = lax.broadcasted_iota(jnp.int32, (order, order), 0)
    columns = lax.broadcasted_iota(jnp.int32, (order, order), 1)
    return jnp.where(rows == columns, 1.0, 0.0).astype(F32)


def newton_inverse(d_high, d_low, x_ref, start):
    order = x_ref.shape[0]

    def rough(state):
        step, size = state
        x = x_ref[...].astype(BF16)
        residual = identity(order) - dot1(d_high[...], x)
        x_ref[...] = x.astype(F32) + dot1(x, residual.astype(BF16))
        return step + 1, jnp.sum(residual * residual)

    _, size = lax.while_loop(
        lambda state: (state[0] < 30) & (state[1] > 2.0), rough, (0, jnp.float32(1e30))
    )

    @pl.when(jnp.logical_not(size <= 2.0))
    def _():
        x_ref[...] = start()

    def fine(state):
        step, size, _ = state
        x = split(x_ref[...])
        residual = identity(order) - dot3((d_high[...], d_low[...]), x)
        now = jnp.sum(residual * residual)
        r = residual.astype(BF16)

        @pl.when(now > 1.0)
        def _():
            y = split(residual)
            x_ref[...] = x_ref[...] + (dot1(x[0], y[0]) + (dot1(x[1], y[0]) + dot1(x[0], y[1])))

        @pl.when(now <= 1.0)
        def _():
            square = dot1(r, r)
            series = residual + square + dot1(r, square.astype(BF16))
            x_ref[...] = x_ref[...] + dot1(x[0], series.astype(BF16))

        return step + 1, now, size

    def going(state):
        step, size, before = state
        stalled = (size < 0.1) & (size > 0.25 * before)
        return (step < 60) & (size > 0.02) & jnp.logical_not(stalled)

    lax.while_loop(going, fine, (0, jnp.float32(1e30), jnp.float32(1e30)))


T = 128


def upper_blocks(count):
    return [(i, j) for i in range(count) for j in range(i, count)]


def pack(out, w, u, thin):
    size = thin.shape[0]
    slot = 0
    for i in range(size // T):
        rows = slice(i * T, (i + 1) * T)
        strip = dot3((w[0][rows], w[1][rows]), (u[0][i * T :], u[1][i * T :]), NT)
        for j in range(i, size // T):
            out[slot * T : (slot + 1) * T, :] = strip[:, (j - i) * T : (j - i + 1) * T]
            slot += 1
    out[slot * T :, :] = thin


def total(updates, rows):
    out = updates[0][rows, :]
    for update in updates[1:]:
        out = out + update[rows, :]
    return out


def subtract_packed(d_ref, updates, d_out):
    count = d_ref.shape[0] // T
    for slot, (i, j) in enumerate(upper_blocks(count)):
        here = slice(slot * T, (slot + 1) * T)
        block = total(updates, here)
        rows, columns = slice(i * T, (i + 1) * T), slice(j * T, (j + 1) * T)
        d_out[rows, columns] = d_ref[rows, columns] - block
        if i != j:
            d_out[columns, rows] = d_ref[columns, rows] - block.T
    return (slot + 1) * T


def inverse_kernel(first, *refs):
    if first:
        d_ref, load_ref, order_ref, v_ref, g_ref, b_out, d_high, d_low = refs
        size = load_ref.shape[0]
        d = d_ref[...]
        places = lax.broadcasted_iota(jnp.int32, (size, size), 0)
        chosen = jnp.where(places == order_ref[...], 1.0, 0.0).astype(BF16)
        load = load_ref[...]
        high = load.astype(BF16)
        rest = load - high.astype(F32)
        middle = rest.astype(BF16)
        low = (rest - middle.astype(F32)).astype(BF16)
        take = (((0,), (0,)), ((), ()))
        b = dot1(chosen, high, take) + (dot1(chosen, middle, take) + dot1(chosen, low, take))
    else:
        d_ref, b_ref, *updates, v_ref, g_ref, d_out, b_out, d_high, d_low = refs
        size = b_ref.shape[0]
        end = subtract_packed(d_ref, updates, d_out)
        d = d_out[...]
        b = b_ref[...] - total(updates, slice(end, None))
    b_out[...] = b
    d_high[...], d_low[...] = split(d)
    scale = 1.9 / jnp.max(jnp.sum(jnp.abs(d), axis=1))

    def start():
        whole = d_high[...].astype(F32) + d_low[...].astype(F32)
        return scale * (2.0 * identity(size) - scale * whole)

    v_ref[...] = start()
    newton_inverse(d_high, d_low, v_ref, start)
    g_ref[...] = dot3(split(v_ref[...]), split(b_out[...]))


def update_kernel(first, v_ref, g_ref, left_ref, right_ref, to_left, to_right, *rest):
    size = v_ref.shape[0]
    v = split(v_ref[...])
    g = split(g_ref[...])
    right = right_ref[...]
    if first:
        at_end = lax.axis_index("chain") == lax.axis_size("chain") - 1
        right = jnp.where(at_end, 0.0, right.T)
        rest[0][...] = right
    for coupling, out in ((right, to_right), (left_ref[...], to_left)):
        u = split(coupling)
        w = split(dot3(u, v))
        pack(out, w, u, dot3(u, g))


def couple_kernel(passed, v_ref, left_ref, right_ref, h_ref, m_ref, *rest):
    v = split(v_ref[...])
    left = split(left_ref[...])
    right = split(right_ref[...])
    h = dot3(v, left, NT)
    m = dot3(v, right, NT)
    h_ref[...] = h
    m_ref[...] = m
    if passed:
        onward, back = rest
        onward[...] = -dot3(left, split(m))
        back[...] = -dot3(right, split(h))


def sweep_kernel(strides, devices, *refs):
    count = len(strides)
    x_in = refs[0]
    kept = [refs[1 + 3 * k : 4 + 3 * k] for k in range(count)]
    spike_left, spike_right, local, x_ref, out_ref = refs[1 + 3 * count : 6 + 3 * count]
    slots, own, given, send_sem, recv_sem, load_sem = refs[6 + 3 * count : 12 + 3 * count]
    buffers = refs[12 + 3 * count :]
    loads = []
    for source in (*(ref for k in reversed(range(count)) for ref in kept[k]), spike_right, spike_left, local):
        at = len(loads)
        loads.append(pltpu.make_async_copy(source, buffers[at], load_sem.at[at]))
        loads[-1].start()
    me = lax.axis_index("chain")

    def along(distance):
        return lax.rem(me + (distance + devices), devices)

    def roles(k):
        stride, at_ends = strides[k]
        if at_ends:
            return me == 3 * stride, me == 0, me == 2 * stride, me == stride
        place = lax.rem(me, 2 * stride)
        gone, stays = place == stride, place == 0
        return gone, gone & (me + stride < devices), stays, stays & (me >= stride)

    def copies(k):
        stride = strides[k][0]
        rightward = pltpu.make_async_remote_copy(
            x_ref,
            slots.at[2 * k],
            send_sem.at[2 * k],
            recv_sem.at[2 * k],
            device_id={"chain": along(stride)},
            device_id_type=pl.DeviceIdType.MESH,
        )
        leftward = pltpu.make_async_remote_copy(
            x_ref,
            slots.at[2 * k + 1],
            send_sem.at[2 * k + 1],
            recv_sem.at[2 * k + 1],
            device_id={"chain": along(-stride)},
            device_id_type=pl.DeviceIdType.MESH,
        )
        return rightward, leftward

    round_copy = pltpu.make_async_remote_copy(
        own,
        given,
        send_sem.at[2 * count],
        recv_sem.at[2 * count],
        device_id={"chain": along(1)},
        device_id_type=pl.DeviceIdType.MESH,
    )
    x_ref[...] = x_in[...]
    slots[...] = jnp.zeros_like(slots)
    barrier = pltpu.get_barrier_semaphore()
    partners = jnp.int32(0)
    for k in range(count):
        takes_left, takes_right, gives_right, gives_left = roles(k)
        stride = strides[k][0]
        for meets, distance in ((takes_left | gives_left, -stride), (takes_right | gives_right, stride)):
            partners = partners + meets.astype(jnp.int32)

            @pl.when(meets)
            def _():
                pl.semaphore_signal(
                    barrier,
                    inc=1,
                    device_id={"chain": along(distance)},
                    device_id_type=pl.DeviceIdType.MESH,
                )

    pl.semaphore_wait(barrier, partners)
    for k in reversed(range(count)):
        takes_left, takes_right, gives_right, gives_left = roles(k)
        rightward, leftward = copies(k)
        pl.when(gives_right)(rightward.start)
        pl.when(gives_left)(leftward.start)
        pl.when(takes_left)(rightward.wait_recv)
        pl.when(takes_right)(leftward.wait_recv)
        first = 3 * (count - 1 - k)
        for at in range(first, first + 3):
            loads[at].wait()
        g_ref, h_ref, m_ref = buffers[first : first + 3]

        @pl.when(takes_left | takes_right)
        def _():
            x_ref[...] = g_ref[...] - (
                dot3(split(h_ref[...]), split(slots[2 * k]))
                + dot3(split(m_ref[...]), split(slots[2 * k + 1]))
            )

    own[...] = x_ref[...].astype(BF16)
    odd = lax.rem(me, 2) == 1
    gives, takes = odd & (me < devices - 1), jnp.logical_not(odd) & (me > 0)
    pl.when(gives)(round_copy.start)
    for at in range(3 * count, 3 * count + 3):
        loads[at].wait()
    spike_right, spike_left, local = buffers[3 * count :]
    out_ref[...] = dot1(spike_right[...], own[...])

    @pl.when(odd)
    def _():
        given[...] = slots[0].astype(BF16)

    @pl.when(me == 0)
    def _():
        given[...] = jnp.zeros_like(given)

    pl.when(takes)(round_copy.wait_recv)
    out_ref[...] = local[...] - (dot1(spike_left[...], given[...]) + out_ref[...])
    pl.when(gives)(round_copy.wait_send)
    for k in range(count):
        _, _, gives_right, gives_left = roles(k)
        rightward, leftward = copies(k)
        pl.when(gives_right)(rightward.wait_send)
        pl.when(gives_left)(leftward.wait_send)


def call(kernel, out_shape, *operands, scratch=(), flops=0, far=0, **params):
    return pl.pallas_call(
        kernel,
        out_shape=out_shape,
        in_specs=[pl.BlockSpec(memory_space=pltpu.VMEM)] * (len(operands) - far)
        + [pl.BlockSpec(memory_space=pl.ANY)] * far,
        out_specs=jax.tree.map(lambda _: pl.BlockSpec(memory_space=pltpu.VMEM), out_shape),
        scratch_shapes=list(scratch),
        compiler_params=pltpu.CompilerParams(vmem_limit_bytes=48 * 2**20, **params),
        cost_estimate=pl.CostEstimate(flops=flops, bytes_accessed=4 * 2**20, transcendentals=0),
    )(*operands)


def send(block, distance, senders, devices):
    route = [(i, i + distance) for i in senders if 0 <= i + distance < devices]
    return lax.ppermute(block, "chain", route)


def plan(devices):
    levels = []
    stride = 1
    while devices // stride > 4:
        levels.append((stride, list(range(stride, devices, 2 * stride))))
        stride *= 2
    return levels, stride


def per_device(
    separator_block, coupling, separator_load, node_order, spike_left, spike_right, interior_local
):
    devices = lax.axis_size("chain")
    size = separator_block.shape[1]
    wide = separator_load.shape[2]
    square = jax.ShapeDtypeStruct((size, size), F32)
    thin = jax.ShapeDtypeStruct((size, wide), F32)
    payload = jax.ShapeDtypeStruct((len(upper_blocks(size // T)) * T + size, wide), F32)
    halves = (pltpu.VMEM((size, size), BF16),) * 2
    cube = 2 * size**3

    d = separator_block[0]
    right = coupling[0]
    levels, top = plan(devices)
    left = send(right, 1, [i - 1 for i in levels[0][1]], devices)

    def invert(d, b, updates):
        return call(
            functools.partial(inverse_kernel, False),
            (square, thin, square, thin),
            d,
            b,
            *updates,
            scratch=halves,
            flops=16 * cube,
        )

    def update(first, v, g, left, right):
        return call(
            functools.partial(update_kernel, first),
            (payload, payload) + ((square,) if first else ()),
            v,
            g,
            left,
            right,
            flops=12 * cube,
        )

    def couple(passed, v, left, right):
        return call(
            functools.partial(couple_kernel, passed),
            (square, square) + ((square, square) if passed else ()),
            v,
            left,
            right,
            flops=12 * cube,
        )

    kept = []
    b = None
    updates = ()
    for index, (stride, gone) in enumerate(levels):
        first = index == 0
        if first:
            v, g, b = call(
                functools.partial(inverse_kernel, True),
                (square, thin, thin),
                d,
                separator_load[0],
                node_order.reshape(1, size),
                scratch=halves,
                flops=16 * cube,
            )
        else:
            v, g, d, b = invert(d, b, updates)
        outs = update(first, v, g, left, right)
        to_left, to_right = outs[:2]
        if first:
            right = outs[2]
        before_top = 2 * stride == top
        if before_top:
            urgent_left, urgent_right = [gone[0], gone[1], gone[3]], [gone[1], gone[2]]
            coupled_right, coupled_left = [gone[1], gone[2]], [gone[0], gone[1]]
        else:
            urgent_left, urgent_right = gone, gone
            coupled_right, coupled_left = gone[0::2], gone[1::2]
        updates = (
            send(to_left, -stride, urgent_left, devices),
            send(to_right, stride, urgent_right, devices),
        )
        h, m, onward, back = couple(True, v, left, right)
        kept.append((g, h, m))
        if before_top:
            onward, back, *updates = lax.optimization_barrier((onward, back, *updates))
        left = send(onward, stride, coupled_right, devices)
        right = send(back, -stride, coupled_left, devices)

    left, right, to_left, to_right = lax.optimization_barrier((left, right, to_left, to_right))
    later = (
        send(to_left, -(top // 2), [5 * top // 2], devices),
        send(to_right, top // 2, [top // 2], devices),
    )
    v, g, d, b = invert(d, b, updates)
    to_left, to_right = update(False, v, g, left, right)
    updates = (
        send(to_left, -top, [3 * top], devices),
        send(to_right, top, [0], devices),
    )
    h, m = couple(False, v, left, right)
    kept.append((g, h, m))

    v, g, d, b = invert(d, b, (*later, *updates))
    to_left, to_right = update(False, v, g, left, right)
    updates = (
        send(to_left, -top, [2 * top], devices),
        send(to_right, top, [top], devices),
    )
    _, x, _, _ = invert(d, b, updates)

    strides = [(stride, False) for stride, _ in levels] + [(top, True)]
    tall = interior_local.shape[1]
    x, interior = call(
        functools.partial(sweep_kernel, strides, devices),
        (thin, jax.ShapeDtypeStruct((tall, wide), F32)),
        x,
        *(array for entry in kept for array in entry),
        spike_left[0],
        spike_right[0],
        interior_local[0],
        scratch=(
            pltpu.VMEM((2 * len(strides), size, wide), F32),
            pltpu.VMEM((size, wide), BF16),
            pltpu.VMEM((size, wide), BF16),
            pltpu.SemaphoreType.DMA((2 * len(strides) + 1,)),
            pltpu.SemaphoreType.DMA((2 * len(strides) + 1,)),
            pltpu.SemaphoreType.DMA((3 * len(strides) + 3,)),
            *(pltpu.VMEM((size, count), F32) for _ in strides for count in (wide, size, size)),
            pltpu.VMEM((tall, size), BF16),
            pltpu.VMEM((tall, size), BF16),
            pltpu.VMEM((tall, wide), F32),
        ),
        far=3 * len(strides) + 3,
        flops=6 * cube,
        collective_id=0,
        has_side_effects=True,
    )
    return (x[None], interior[None])


def solution(mesh):
    blocks = P(("group", "chain"), None, None)
    placed = (blocks, blocks, blocks, P(("group", "chain"), None), blocks, blocks, blocks)
    return jax.shard_map(
        per_device, mesh=mesh, in_specs=placed, out_specs=(blocks, blocks), check_vma=False
    )
```

```python
import functools

import jax
import jax.numpy as jnp
from jax import lax
from jax.experimental import pallas as pl
from jax.experimental.pallas import tpu as pltpu
from jax.sharding import PartitionSpec as P

F32 = jnp.float32
BF16 = jnp.bfloat16
NN = (((1,), (0,)), ((), ()))
NT = (((1,), (1,)), ((), ()))


def split(a):
    high = a.astype(BF16)
    return high, (a - high.astype(F32)).astype(BF16)


def dot1(a, b, dims=NN):
    return lax.dot_general(a, b, dims, preferred_element_type=F32)


def dot3(a, b, dims=NN):
    return dot1(a[0], b[0], dims) + (dot1(a[0], b[1], dims) + dot1(a[1], b[0], dims))


def identity(order):
    rows = lax.broadcasted_iota(jnp.int32, (order, order), 0)
    columns = lax.broadcasted_iota(jnp.int32, (order, order), 1)
    return jnp.where(rows == columns, 1.0, 0.0).astype(F32)


def newton_inverse(d_high, d_low, x_ref, start):
    order = x_ref.shape[0]

    def rough(state):
        step, size = state
        x = x_ref[...].astype(BF16)
        residual = identity(order) - dot1(d_high[...], x)
        x_ref[...] = x.astype(F32) + dot1(x, residual.astype(BF16))
        return step + 1, jnp.sum(residual * residual)

    _, size = lax.while_loop(
        lambda state: (state[0] < 30) & (state[1] > 2.0), rough, (0, jnp.float32(1e30))
    )

    @pl.when(jnp.logical_not(size <= 2.0))
    def _():
        x_ref[...] = start()

    def fine(state):
        step, size, _ = state
        x = split(x_ref[...])
        residual = identity(order) - dot3((d_high[...], d_low[...]), x)
        now = jnp.sum(residual * residual)
        r = residual.astype(BF16)

        @pl.when(now > 1.0)
        def _():
            y = split(residual)
            x_ref[...] = x_ref[...] + (dot1(x[0], y[0]) + (dot1(x[1], y[0]) + dot1(x[0], y[1])))

        @pl.when(now <= 1.0)
        def _():
            square = dot1(r, r)
            series = residual + square + dot1(r, square.astype(BF16))
            x_ref[...] = x_ref[...] + dot1(x[0], series.astype(BF16))

        return step + 1, now, size

    def going(state):
        step, size, before = state
        stalled = (size < 0.1) & (size > 0.25 * before)
        return (step < 60) & (size > 0.02) & jnp.logical_not(stalled)

    lax.while_loop(going, fine, (0, jnp.float32(1e30), jnp.float32(1e30)))


T = 128


def upper_blocks(count):
    return [(i, j) for i in range(count) for j in range(i, count)]


def pack(out, w, u, thin):
    size = thin.shape[0]
    slot = 0
    for i in range(size // T):
        rows = slice(i * T, (i + 1) * T)
        strip = dot3((w[0][rows], w[1][rows]), (u[0][i * T :], u[1][i * T :]), NT)
        for j in range(i, size // T):
            out[slot * T : (slot + 1) * T, :] = strip[:, (j - i) * T : (j - i + 1) * T]
            slot += 1
    out[slot * T :, :] = thin


def total(updates, rows):
    out = updates[0][rows, :]
    for update in updates[1:]:
        out = out + update[rows, :]
    return out


def subtract_packed(d_ref, updates, d_out):
    count = d_ref.shape[0] // T
    for slot, (i, j) in enumerate(upper_blocks(count)):
        here = slice(slot * T, (slot + 1) * T)
        block = total(updates, here)
        rows, columns = slice(i * T, (i + 1) * T), slice(j * T, (j + 1) * T)
        d_out[rows, columns] = d_ref[rows, columns] - block
        if i != j:
            d_out[columns, rows] = d_ref[columns, rows] - block.T
    return (slot + 1) * T


def inverse_kernel(first, *refs):
    if first:
        d_ref, load_ref, order_ref, v_ref, g_ref, b_out, d_high, d_low = refs
        size = load_ref.shape[0]
        d = d_ref[...]
        places = lax.broadcasted_iota(jnp.int32, (size, size), 0)
        chosen = jnp.where(places == order_ref[...], 1.0, 0.0).astype(BF16)
        load = load_ref[...]
        high = load.astype(BF16)
        rest = load - high.astype(F32)
        middle = rest.astype(BF16)
        low = (rest - middle.astype(F32)).astype(BF16)
        take = (((0,), (0,)), ((), ()))
        b = dot1(chosen, high, take) + (dot1(chosen, middle, take) + dot1(chosen, low, take))
    else:
        d_ref, b_ref, *updates, v_ref, g_ref, d_out, b_out, d_high, d_low = refs
        size = b_ref.shape[0]
        end = subtract_packed(d_ref, updates, d_out)
        d = d_out[...]
        b = b_ref[...] - total(updates, slice(end, None))
    b_out[...] = b
    d_high[...], d_low[...] = split(d)
    scale = 1.9 / jnp.max(jnp.sum(jnp.abs(d), axis=1))

    def start():
        whole = d_high[...].astype(F32) + d_low[...].astype(F32)
        return scale * (2.0 * identity(size) - scale * whole)

    v_ref[...] = start()
    newton_inverse(d_high, d_low, v_ref, start)
    g_ref[...] = dot3(split(v_ref[...]), split(b_out[...]))


def update_kernel(first, v_ref, g_ref, u_ref, out, *rest):
    v = split(v_ref[...])
    u = u_ref[...]
    if first:
        at_end = lax.axis_index("chain") == lax.axis_size("chain") - 1
        u = jnp.where(at_end, 0.0, u.T)
        rest[0][...] = u
    u = split(u)
    pack(out, split(dot3(u, v)), u, dot3(u, split(g_ref[...])))


def one_sided_kernel(rightward, v_ref, g_ref, left_ref, right_ref, out):
    v = split(v_ref[...])
    u = split(jnp.where(lax.axis_index("chain") == rightward, right_ref[...], left_ref[...]))
    pack(out, split(dot3(u, v)), u, dot3(u, split(g_ref[...])))


def couple_kernel(passed, v_ref, left_ref, right_ref, h_ref, m_ref, *rest):
    v = split(v_ref[...])
    left = split(left_ref[...])
    right = split(right_ref[...])
    h = dot3(v, left, NT)
    m = dot3(v, right, NT)
    h_ref[...] = h
    m_ref[...] = m
    if passed:
        onward, back = rest
        onward[...] = -dot3(left, split(m))
        back[...] = -dot3(right, split(h))


def sweep_kernel(strides, devices, *refs):
    count = len(strides)
    x_in = refs[0]
    kept = [refs[1 + 3 * k : 4 + 3 * k] for k in range(count)]
    spike_left, spike_right, local, x_ref, out_ref = refs[1 + 3 * count : 6 + 3 * count]
    slots, own, given, send_sem, recv_sem, load_sem = refs[6 + 3 * count : 12 + 3 * count]
    buffers = refs[12 + 3 * count :]
    loads = []
    for source in (*(ref for k in reversed(range(count)) for ref in kept[k]), spike_right, spike_left, local):
        at = len(loads)
        loads.append(pltpu.make_async_copy(source, buffers[at], load_sem.at[at]))
        loads[-1].start()
    me = lax.axis_index("chain")

    def along(distance):
        return lax.rem(me + (distance + devices), devices)

    def roles(k):
        stride, at_ends = strides[k]
        if at_ends:
            return me == 3 * stride, me == 0, me == 2 * stride, me == stride
        place = lax.rem(me, 2 * stride)
        gone, stays = place == stride, place == 0
        return gone, gone & (me + stride < devices), stays, stays & (me >= stride)

    def copies(k):
        stride = strides[k][0]
        rightward = pltpu.make_async_remote_copy(
            x_ref,
            slots.at[2 * k],
            send_sem.at[2 * k],
            recv_sem.at[2 * k],
            device_id={"chain": along(stride)},
            device_id_type=pl.DeviceIdType.MESH,
        )
        leftward = pltpu.make_async_remote_copy(
            x_ref,
            slots.at[2 * k + 1],
            send_sem.at[2 * k + 1],
            recv_sem.at[2 * k + 1],
            device_id={"chain": along(-stride)},
            device_id_type=pl.DeviceIdType.MESH,
        )
        return rightward, leftward

    round_copy = pltpu.make_async_remote_copy(
        own,
        given,
        send_sem.at[2 * count],
        recv_sem.at[2 * count],
        device_id={"chain": along(1)},
        device_id_type=pl.DeviceIdType.MESH,
    )
    x_ref[...] = x_in[...]
    slots[...] = jnp.zeros_like(slots)
    barrier = pltpu.get_barrier_semaphore()
    partners = jnp.int32(0)
    for k in range(count):
        takes_left, takes_right, gives_right, gives_left = roles(k)
        stride = strides[k][0]
        for meets, distance in ((takes_left | gives_left, -stride), (takes_right | gives_right, stride)):
            partners = partners + meets.astype(jnp.int32)

            @pl.when(meets)
            def _():
                pl.semaphore_signal(
                    barrier,
                    inc=1,
                    device_id={"chain": along(distance)},
                    device_id_type=pl.DeviceIdType.MESH,
                )

    pl.semaphore_wait(barrier, partners)
    for k in reversed(range(count)):
        takes_left, takes_right, gives_right, gives_left = roles(k)
        rightward, leftward = copies(k)
        pl.when(gives_right)(rightward.start)
        pl.when(gives_left)(leftward.start)
        pl.when(takes_left)(rightward.wait_recv)
        pl.when(takes_right)(leftward.wait_recv)
        first = 3 * (count - 1 - k)
        for at in range(first, first + 3):
            loads[at].wait()
        g_ref, h_ref, m_ref = buffers[first : first + 3]

        @pl.when(takes_left | takes_right)
        def _():
            x_ref[...] = g_ref[...] - (
                dot3(split(h_ref[...]), split(slots[2 * k]))
                + dot3(split(m_ref[...]), split(slots[2 * k + 1]))
            )

    own[...] = x_ref[...].astype(BF16)
    odd = lax.rem(me, 2) == 1
    gives, takes = odd & (me < devices - 1), jnp.logical_not(odd) & (me > 0)
    pl.when(gives)(round_copy.start)
    for at in range(3 * count, 3 * count + 3):
        loads[at].wait()
    spike_right, spike_left, local = buffers[3 * count :]
    out_ref[...] = dot1(spike_right[...], own[...])

    @pl.when(odd)
    def _():
        given[...] = slots[0].astype(BF16)

    @pl.when(me == 0)
    def _():
        given[...] = jnp.zeros_like(given)

    pl.when(takes)(round_copy.wait_recv)
    out_ref[...] = local[...] - (dot1(spike_left[...], given[...]) + out_ref[...])
    pl.when(gives)(round_copy.wait_send)
    for k in range(count):
        _, _, gives_right, gives_left = roles(k)
        rightward, leftward = copies(k)
        pl.when(gives_right)(rightward.wait_send)
        pl.when(gives_left)(leftward.wait_send)


def call(kernel, out_shape, *operands, scratch=(), flops=0, far=0, **params):
    return pl.pallas_call(
        kernel,
        out_shape=out_shape,
        in_specs=[pl.BlockSpec(memory_space=pltpu.VMEM)] * (len(operands) - far)
        + [pl.BlockSpec(memory_space=pl.ANY)] * far,
        out_specs=jax.tree.map(lambda _: pl.BlockSpec(memory_space=pltpu.VMEM), out_shape),
        scratch_shapes=list(scratch),
        compiler_params=pltpu.CompilerParams(vmem_limit_bytes=48 * 2**20, **params),
        cost_estimate=pl.CostEstimate(flops=flops, bytes_accessed=4 * 2**20, transcendentals=0),
    )(*operands)


def send(block, distance, senders, devices):
    route = [(i, i + distance) for i in senders if 0 <= i + distance < devices]
    return lax.ppermute(block, "chain", route)


def plan(devices):
    levels = []
    stride = 1
    while devices // stride > 4:
        levels.append((stride, list(range(stride, devices, 2 * stride))))
        stride *= 2
    return levels, stride


def per_device(
    separator_block, coupling, separator_load, node_order, spike_left, spike_right, interior_local
):
    devices = lax.axis_size("chain")
    size = separator_block.shape[1]
    wide = separator_load.shape[2]
    square = jax.ShapeDtypeStruct((size, size), F32)
    thin = jax.ShapeDtypeStruct((size, wide), F32)
    payload = jax.ShapeDtypeStruct((len(upper_blocks(size // T)) * T + size, wide), F32)
    halves = (pltpu.VMEM((size, size), BF16),) * 2
    cube = 2 * size**3

    d = separator_block[0]
    right = coupling[0]
    levels, top = plan(devices)
    left = send(right, 1, [i - 1 for i in levels[0][1]], devices)

    def invert(d, b, updates):
        return call(
            functools.partial(inverse_kernel, False),
            (square, thin, square, thin),
            d,
            b,
            *updates,
            scratch=halves,
            flops=16 * cube,
        )

    def update(first, v, g, coupling):
        return call(
            functools.partial(update_kernel, first),
            (payload,) + ((square,) if first else ()),
            v,
            g,
            coupling,
            flops=6 * cube,
        )

    def swap(v, g, left, right, giver, other):
        given = call(
            functools.partial(one_sided_kernel, giver), payload, v, g, left, right, flops=6 * cube
        )
        return lax.ppermute(given, "chain", [(giver, giver + top), (other, other - top)])

    def couple(passed, v, left, right):
        return call(
            functools.partial(couple_kernel, passed),
            (square, square) + ((square, square) if passed else ()),
            v,
            left,
            right,
            flops=12 * cube,
        )

    kept = []
    b = None
    updates = ()
    for index, (stride, gone) in enumerate(levels):
        first = index == 0
        if first:
            v, g, b = call(
                functools.partial(inverse_kernel, True),
                (square, thin, thin),
                d,
                separator_load[0],
                node_order.reshape(1, size),
                scratch=halves,
                flops=16 * cube,
            )
        else:
            v, g, d, b = invert(d, b, updates)
        outs = update(first, v, g, right)
        to_right = outs[0]
        if first:
            right = outs[1]
        (to_left,) = update(False, v, g, left)
        before_top = 2 * stride == top
        if before_top:
            urgent_left, urgent_right = [gone[0], gone[1], gone[3]], [gone[1], gone[2]]
            coupled_right, coupled_left = [gone[1], gone[2]], [gone[0], gone[1]]
        else:
            urgent_left, urgent_right = gone, gone
            coupled_right, coupled_left = gone[0::2], gone[1::2]
        from_left = send(to_right, stride, urgent_right, devices)
        updates = (send(to_left, -stride, urgent_left, devices), from_left)
        h, m, onward, back = couple(True, v, left, right)
        kept.append((g, h, m))
        if before_top:
            onward, back, *updates = lax.optimization_barrier((onward, back, *updates))
        left = send(onward, stride, coupled_right, devices)
        right = send(back, -stride, coupled_left, devices)

    left, right, to_left, to_right = lax.optimization_barrier((left, right, to_left, to_right))
    later = (
        send(to_left, -(top // 2), [5 * top // 2], devices),
        send(to_right, top // 2, [top // 2], devices),
    )
    v, g, d, b = invert(d, b, updates)
    updates = (swap(v, g, left, right, 0, 3 * top),)
    h, m = couple(False, v, left, right)
    kept.append((g, h, m))

    v, g, d, b = invert(d, b, (*later, *updates))
    updates = (swap(v, g, left, right, top, 2 * top),)
    _, x, _, _ = invert(d, b, updates)

    strides = [(stride, False) for stride, _ in levels] + [(top, True)]
    tall = interior_local.shape[1]
    x, interior = call(
        functools.partial(sweep_kernel, strides, devices),
        (thin, jax.ShapeDtypeStruct((tall, wide), F32)),
        x,
        *(array for entry in kept for array in entry),
        spike_left[0],
        spike_right[0],
        interior_local[0],
        scratch=(
            pltpu.VMEM((2 * len(strides), size, wide), F32),
            pltpu.VMEM((size, wide), BF16),
            pltpu.VMEM((size, wide), BF16),
            pltpu.SemaphoreType.DMA((2 * len(strides) + 1,)),
            pltpu.SemaphoreType.DMA((2 * len(strides) + 1,)),
            pltpu.SemaphoreType.DMA((3 * len(strides) + 3,)),
            *(pltpu.VMEM((size, count), F32) for _ in strides for count in (wide, size, size)),
            pltpu.VMEM((tall, size), BF16),
            pltpu.VMEM((tall, size), BF16),
            pltpu.VMEM((tall, wide), F32),
        ),
        far=3 * len(strides) + 3,
        flops=6 * cube,
        collective_id=0,
        has_side_effects=True,
    )
    return (x[None], interior[None])


def solution(mesh):
    blocks = P(("group", "chain"), None, None)
    placed = (blocks, blocks, blocks, P(("group", "chain"), None), blocks, blocks, blocks)
    return jax.shard_map(
        per_device, mesh=mesh, in_specs=placed, out_specs=(blocks, blocks), check_vma=False
    )
```
